32 devices in a mesh: pipe: 2 (over x), fsdp: 8 (over z, y), rep: 2 (over core).
Axes of the slice: x: 2, y: 2, z: 4, core: 2. Of those that a mesh axis runs over, the one named last changes fastest.
Arguments:
- section_acts: bfloat16 [2, 2, 1024, 3072], P('pipe', 'rep', 'fsdp'), may hold values from -6 to 6
- route_ids: int32 [2, 2, 1024, 2], P('pipe', 'rep', 'fsdp'), may hold values from 0 to 7, as said below
- gate_weight: bfloat16 [2, 3072, 8192], P('pipe', None, 'fsdp'), may hold values from -0.109375 to 0.109375
- hidden_cot: bfloat16 [2, 2, 192, 8192], P('pipe', 'rep', None, 'fsdp'), may hold values from -6 to 6
Outputs:
- weight_grad: bfloat16 [2, 3072, 8192], P('pipe', 'rep', 'fsdp')
- acts_grad: bfloat16 [2, 2, 1024, 3072], P('pipe', 'rep', 'fsdp')
The draws below stay inside these ranges and needn't reach their ends.
Inputs may be any that keep to these rules, and one draw needn't show every extreme that they name: `route_ids`: in every section, replica and block of 128 consecutive tokens at most 24 tokens name expert 0, and in every section and replica some block has exactly 24; a token's two ids differ.
All inputs are finite; a program needn't handle non-finite values.
Results may differ from the reference program's by a relative error of at most 0.0059.
Values may be sent and summed in bfloat16 or wider, within the bound.
A program may use at most 128 MiB of HBM per device.

```python
import jax
import jax.numpy as jnp

D = 3072
FF = 8192
EXPERTS = 8
TOPK = 2
TOK_DEV = 128
CAP = 24
SECTIONS = 2
REPLICAS = 2
TOKENS = 1024
SLOTS = 192


def draw_route_ids(key, part):
    subkeys = jax.random.split(jax.random.fold_in(key, 17), 6)
    blocks = TOKENS // TOK_DEV
    levels_table = jnp.array([CAP, CAP // 2, CAP // 3, CAP // 4], jnp.int32)
    levels = jax.random.randint(subkeys[0], (SECTIONS, REPLICAS, blocks), 0, 4)
    counts = levels_table[levels]
    chosen = jax.random.randint(subkeys[1], (SECTIONS, REPLICAS, 1), 0, blocks)
    counts = jnp.where(jnp.arange(blocks, dtype=jnp.int32)[None, None, :] == chosen, CAP, counts)
    shape = (SECTIONS, REPLICAS, blocks, TOK_DEV)
    scores = jax.random.randint(subkeys[2], shape, 0, 2 ** 20) * TOK_DEV + jnp.arange(TOK_DEV, dtype=jnp.int32)
    ranking = jnp.argsort(jnp.argsort(scores, axis=-1, stable=True), axis=-1, stable=True)
    routed = ranking < counts[..., None]
    placed = jax.random.randint(subkeys[3], shape, 0, 2)
    partner = jax.random.randint(subkeys[4], shape, 1, EXPERTS)
    offset = jax.random.randint(subkeys[5], shape, 1, EXPERTS - 1)
    second = 1 + (partner - 1 + offset) % (EXPERTS - 1)
    leading = jnp.where(routed, 0, partner)
    trailing = jnp.where(routed, partner, second)
    column_a = jnp.where(placed == 0, leading, trailing)
    column_b = jnp.where(placed == 0, trailing, leading)
    stacked = jnp.stack([column_a, column_b], axis=-1)
    return stacked.reshape(SECTIONS, REPLICAS, TOKENS, TOPK).astype(jnp.int32)


def steps_of(rng, dims, pieces, smallest, high):
    def one(dim, blocks):
        heights = jax.random.uniform(jax.random.fold_in(jax.random.fold_in(rng, 6), dim), (blocks,), jnp.float32, smallest / len(pieces), high / len(pieces))
        return jnp.repeat(jnp.exp(heights), dims[dim] // blocks).reshape((-1,) + (1,) * (len(dims) - dim - 1))

    gain = one(*pieces[0])
    for cut in pieces[1:]:
        gain = gain * one(*cut)
    return gain


def gaussian(key, dims, width, reach, pieces=(), held_as=jnp.bfloat16):
    entries = width * jax.random.normal(key, dims, jnp.float32)
    if pieces:
        entries = entries * steps_of(key, dims, pieces, -0.22, 0.18)
    return jnp.clip(entries, -reach, reach).astype(held_as)


def setup_inputs(seed: int = 0) -> dict:
    key_list = jax.random.split(jax.random.key(seed), 5)
    section_acts = gaussian(key_list[0], (SECTIONS, REPLICAS, TOKENS, D), 1.0, 6.0, ((0, 2), (1, 2), (2, 8)))
    route_ids = draw_route_ids(jax.random.fold_in(key_list[4], 71), 0)
    gate_weight = gaussian(key_list[2], (SECTIONS, D, FF), D ** -0.5, 0.109375, ((0, 2), (2, 8)))
    hidden_cot = gaussian(key_list[3], (SECTIONS, REPLICAS, SLOTS, FF), 1.0, 6.0, ((0, 2), (1, 2), (3, 8)))
    return {"section_acts": section_acts, "route_ids": route_ids, "gate_weight": gate_weight, "hidden_cot": hidden_cot}


def slot_pick(route_block, capacity):
    chosen = jnp.any(route_block == 0, axis=-1)
    ordinal = jnp.cumsum(chosen.astype(jnp.int32), axis=-1) - 1
    slot_ids = jnp.arange(capacity, dtype=jnp.int32)
    hits = (ordinal[..., None, :] == slot_ids[:, None]) & chosen[..., None, :]
    return hits.astype(jnp.float32)


def reference(section_acts, route_ids, gate_weight, hidden_cot):
    groups = TOKENS // TOK_DEV
    weight_grads = []
    input_grads = [[None] * REPLICAS for _ in range(SECTIONS)]
    for section_index in range(SECTIONS):
        weight = gate_weight[section_index]
        weight_sum = jnp.zeros((D, FF), jnp.float32)
        previous = (section_index - 1) % SECTIONS
        for replica in range(REPLICAS):
            inputs = section_acts[previous, replica].reshape(groups, TOK_DEV, D).astype(jnp.float32)
            picker = slot_pick(route_ids[section_index, replica].reshape(groups, TOK_DEV, TOPK), CAP)
            routed = jnp.einsum("gct,gtd->gcd", picker, inputs).reshape(SLOTS, D).astype(jnp.bfloat16)
            pre_act = jnp.dot(routed, weight, preferred_element_type=jnp.float32)
            sig_val = jax.nn.sigmoid(pre_act)
            pre_grad = (hidden_cot[section_index, replica].astype(jnp.float32) * sig_val * (1.0 + pre_act * (1.0 - sig_val))).astype(jnp.bfloat16)
            replica_term = jnp.dot(routed.T, pre_grad, preferred_element_type=jnp.float32).astype(jnp.bfloat16)
            weight_sum = weight_sum + replica_term.astype(jnp.float32)
            slot_grad = jnp.dot(pre_grad, weight.T, preferred_element_type=jnp.float32).astype(jnp.bfloat16)
            slot_grad = slot_grad.reshape(groups, CAP, D).astype(jnp.float32)
            spread = jnp.einsum("gct,gcd->gtd", picker, slot_grad).reshape(TOKENS, D).astype(jnp.bfloat16)
            input_grads[previous][replica] = spread
        weight_grads.append(weight_sum.astype(jnp.bfloat16))
    acts_grad = jnp.stack([jnp.stack(per_section) for per_section in input_grads])
    return (jnp.stack(weight_grads), acts_grad)
```

```python
import functools

import jax
import jax.numpy as jnp
from jax import lax
from jax.experimental import pallas as pl
from jax.experimental.pallas import tpu as pltpu
from jax.sharding import PartitionSpec as P

MESH = pl.DeviceIdType.MESH
F32 = jnp.float32
BF16 = jnp.bfloat16
CHUNKS = 4


def factors(n):
    fast = 1
    while (fast * 2) ** 2 <= n:
        fast *= 2
    return n // fast, fast


def kernel(
    n, pipe, cap,
    routes_hbm, acts_hbm, weight_hbm, cot_hbm,
    wgrad_hbm, agrad_hbm,
    ids, acts, weight, cot, compacted, gathered, rows, acc, pre_grad,
    own_term, y_out, y_in, z_out, up_in, down_in, total, done, back, spread,
    w_out, w_in, w_sum,
    local_sem, ids_sem, x_send, g_recv, g_send, y_send, y_recv, z_send, z_recv,
    b_send, b_recv, w_send, w_recv, o_sem,
):
    chunks = CHUNKS
    slow, fast = factors(n)
    p, f, r = lax.axis_index("pipe"), lax.axis_index("fsdp"), lax.axis_index("rep")
    a, b = f // fast, lax.rem(f, fast)
    nxt, prv = lax.rem(p + 1, pipe), lax.rem(p + pipe - 1, pipe)
    slots = n * cap
    dc = weight.shape[1]
    half = chunks // 2
    has_up, has_down = a < slow - 1, a > 0
    up, down = (a + 1) * fast + b, (a - 1) * fast + b

    def peer(j):
        return a * fast + lax.rem(b + j, fast)

    def remote(src, dst, send, recv, where):
        return pltpu.make_async_remote_copy(
            src_ref=src, dst_ref=dst, send_sem=send, recv_sem=recv,
            device_id=where, device_id_type=MESH,
        )

    def greet(where):
        pl.semaphore_signal(barrier, inc=1, device_id=where, device_id_type=MESH)

    acts_load = pltpu.make_async_copy(acts_hbm, acts, local_sem.at[0])
    acts_load.start()
    barrier = pltpu.get_barrier_semaphore()
    greet({"pipe": prv})
    if pipe > 2:
        greet({"pipe": nxt})
    greet({"rep": 1 - r})
    for j in range(1, fast):
        greet({"fsdp": peer(j)})

    @pl.when(has_up)
    def _():
        greet({"fsdp": up})

    @pl.when(has_down)
    def _():
        greet({"fsdp": down})

    weight_loads = []
    for c in range(chunks):
        load = pltpu.make_async_copy(
            weight_hbm.at[pl.ds(c * dc, dc)], weight.at[c], local_sem.at[2 + c]
        )
        load.start()
        weight_loads.append(load)
    cot_load = pltpu.make_async_copy(cot_hbm, cot, local_sem.at[1])
    cot_load.start()

    greeted = (1 if pipe == 2 else 2) + 1 + (fast - 1)
    pl.semaphore_wait(
        barrier, greeted + has_up.astype(jnp.int32) + has_down.astype(jnp.int32)
    )

    ids_copy = remote(routes_hbm, ids, ids_sem.at[0], ids_sem.at[1], {"pipe": prv})
    ids_copy.start()
    ids_copy.wait_recv()
    tokens = ids.shape[1]
    named = jnp.where(ids[...] == 0, 1.0, 0.0).astype(F32)
    chosen = jnp.max(named, axis=0, keepdims=True)
    row = lax.broadcasted_iota(jnp.int32, (tokens, tokens), 0)
    col = lax.broadcasted_iota(jnp.int32, (tokens, tokens), 1)
    before = jnp.where(row <= col, 1.0, 0.0).astype(BF16)
    chosen8 = jnp.broadcast_to(chosen, (16, tokens))
    ordinal = jnp.dot(chosen8.astype(BF16), before, preferred_element_type=F32)[0:1] - 1.0
    hits = jnp.where(
        (jnp.broadcast_to(ordinal, (tokens, tokens)) == row.astype(F32))
        & (jnp.broadcast_to(chosen, (tokens, tokens)) > 0.5),
        1.0, 0.0,
    ).astype(F32)
    picker = hits[0:cap].astype(BF16)
    spreader = hits.T.astype(BF16)
    acts_load.wait()

    def x_copy(c):
        return remote(
            compacted.at[c], gathered.at[c, f], x_send.at[c], g_recv.at[c, f], {"pipe": nxt}
        )

    for c in range(chunks):
        compacted[c] = jnp.dot(
            picker, acts[:, c * dc:(c + 1) * dc], preferred_element_type=F32
        ).astype(BF16)
        x_copy(c).start()

    def g_copy(c, origin, kind, where):
        block = origin * fast + b
        return remote(
            gathered.at[c, block], gathered.at[c, block],
            g_send.at[c, origin, kind], g_recv.at[c, block], {"fsdp": where},
        )

    def g_wait(c, block):
        remote(
            gathered.at[c, block], gathered.at[c, block],
            g_send.at[c, 0, 0], g_recv.at[c, block], {"pipe": nxt},
        ).wait_recv()

    def g_fan(c, origin, act):
        for j in range(1, fast):
            act(g_copy(c, origin, 1 + j, peer(j)))

    def g_step(c, k, act, wait):
        if k == 0:
            if wait:
                g_wait(c, f)

            @pl.when(has_up)
            def _():
                act(g_copy(c, a, 0, up))

            @pl.when(has_down)
            def _():
                act(g_copy(c, a, 1, down))

            g_fan(c, a, act)
            return

        @pl.when(a - k >= 0)
        def _():
            if wait:
                g_wait(c, (a - k) * fast + b)

            @pl.when(has_up)
            def _():
                act(g_copy(c, a - k, 0, up))

            g_fan(c, a - k, act)

        @pl.when(a + k < slow)
        def _():
            if wait:
                g_wait(c, (a + k) * fast + b)

            @pl.when(has_down)
            def _():
                act(g_copy(c, a + k, 1, down))

            g_fan(c, a + k, act)

    def first_matmul(c):
        for origin in range(slow):
            for j in range(1, fast):
                g_wait(c, origin * fast + lax.rem(b + j, fast))
        block = gathered[c].astype(F32).reshape(slots, dc).astype(BF16)
        rows[c] = block
        weight_loads[c].wait()
        part = jnp.dot(block, weight[c], preferred_element_type=F32)
        if c == 0:
            acc[...] = part
        else:
            acc[...] += part

    for t in range(chunks + slow - 1):
        for c in range(chunks):
            if 0 <= t - c < slow:
                g_step(c, t - c, lambda copy: copy.start(), True)
        c = t - slow + 1
        if c >= 0:
            first_matmul(c)

    cot_load.wait()
    piece = 48
    for i in range(slots // piece):
        span = pl.ds(i * piece, piece)
        pre = acc[span]
        s = jax.nn.sigmoid(pre)
        pre_grad[span] = (cot[span].astype(F32) * s * (1.0 + pre * (1.0 - s))).astype(BF16)

    def y_copy(c, j):
        to = lax.rem(b + j, fast)
        return remote(
            y_out.at[c, to], y_in.at[c, j - 1], y_send.at[c, j - 1], y_recv.at[c, j - 1],
            {"fsdp": peer(j)},
        )

    def slot_matmul(c):
        term = lax.dot_general(
            pre_grad[...], weight[c], (((1,), (1,)), ((), ())), preferred_element_type=F32
        ).reshape(n, cap, dc)
        own_term[c] = term
        for aa in range(slow):
            for bb in range(fast):
                y_out[c, bb, aa] = term[aa * fast + bb].astype(BF16)
        for j in range(1, fast):
            y_copy(c, j).start()

    def partial(c, dest):
        value = own_term[c, dest * fast + b]
        for j in range(1, fast):
            value = value + y_in[c, j - 1, dest].astype(F32)
        return value

    def z_copy(c, dest, way):
        landing = up_in if way == 0 else down_in
        return remote(
            z_out.at[c, dest], landing.at[c, dest], z_send.at[c, dest],
            z_recv.at[way, c, dest], {"fsdp": up if way == 0 else down},
        )

    def z_wait(c, dest, way):
        z_copy(c, dest, way).wait_recv()

    def line(c, dest, way):
        landing = up_in if way == 0 else down_in
        middle = has_down if way == 0 else has_up

        @pl.when(middle)
        def _():
            z_wait(c, dest, way)
            z_out[c, dest] = (partial(c, dest) + landing[c, dest].astype(F32)).astype(BF16)

        @pl.when(jnp.logical_not(middle))
        def _():
            z_out[c, dest] = partial(c, dest).astype(BF16)

        z_copy(c, dest, way).start()

    def back_copy(c):
        return remote(done.at[c], back.at[c], b_send.at[c], b_recv.at[c], {"pipe": prv})

    def r_step(c, k):
        if k == 0:
            for j in range(1, fast):
                y_copy(c, j).wait_recv()
        if k < slow - 1:
            top, bottom = slow - 1 - k, k

            @pl.when(top > a)
            def _():
                line(c, top, 0)

            @pl.when(bottom < a)
            def _():
                line(c, bottom, 1)

            return
        total[...] = partial(c, a)

        @pl.when(has_down)
        def _():
            z_wait(c, a, 0)
            total[...] += up_in[c, a].astype(F32)

        @pl.when(has_up)
        def _():
            z_wait(c, a, 1)
            total[...] += down_in[c, a].astype(F32)

        done[c] = total[...].astype(BF16)
        back_copy(c).start()

    def weight_tile(index):
        return lax.dot_general(
            rows[index], pre_grad[...], (((0,), (0,)), ((), ())), preferred_element_type=F32
        ).astype(BF16)

    def w_copy(i):
        return remote(w_out.at[i], w_in.at[i], w_send.at[i], w_recv.at[i], {"rep": 1 - r})

    def other_half(i):
        w_out[i] = weight_tile((1 - r) * half + i)
        w_copy(i).start()

    def own_half(i):
        w_sum[i] = weight_tile(r * half + i)

    def w_store(i):
        return pltpu.make_async_copy(
            w_sum.at[i], wgrad_hbm.at[pl.ds(i * dc, dc)], o_sem.at[chunks + i]
        )

    def add_halves(i):
        w_copy(i).wait_recv()
        w_sum[i] = (w_sum[i].astype(F32) + w_in[i].astype(F32)).astype(BF16)
        w_store(i).start()

    def a_store(c):
        return pltpu.make_async_copy(
            spread.at[c], agrad_hbm.at[:, pl.ds(c * dc, dc)], o_sem.at[c]
        )

    def put_back(c):
        back_copy(c).wait_recv()
        grads = back[c].astype(F32)
        padded = jnp.concatenate(
            [grads, jnp.zeros((tokens - cap, dc), F32)], axis=0
        ).astype(BF16)
        spread[c] = jnp.dot(spreader, padded, preferred_element_type=F32).astype(BF16)
        a_store(c).start()

    for c in range(chunks):
        slot_matmul(c)
    beside = [functools.partial(other_half, i) for i in range(half)]
    beside += [functools.partial(own_half, i) for i in range(half)]
    beside += [functools.partial(add_halves, i) for i in range(half)]
    for t in range(chunks + slow - 1):
        for c in range(chunks):
            if 0 <= t - c < slow:
                r_step(c, t - c)
        if beside:
            beside.pop(0)()
    for act in beside:
        act()
    for c in range(chunks):
        put_back(c)

    ids_copy.wait_send()
    for c in range(chunks):
        x_copy(c).wait_send()
        for k in range(slow):
            g_step(c, k, lambda copy: copy.wait_send(), False)
        for j in range(1, fast):
            y_copy(c, j).wait_send()
        for dest in range(slow):

            @pl.when(dest != a)
            def _():
                z_copy(c, dest, 0).wait_send()

        back_copy(c).wait_send()
    for i in range(half):
        w_copy(i).wait_send()
        w_store(i).wait()
    for c in range(chunks):
        a_store(c).wait()


def per_device(section_acts, route_ids, gate_weight, hidden_cot):
    n, pipe = lax.axis_size("fsdp"), lax.axis_size("pipe")
    acts, weight, cot = section_acts[0, 0], gate_weight[0], hidden_cot[0, 0]
    routes = route_ids[0, 0].T
    tokens, width = acts.shape
    slots, hidden = cot.shape
    cap = slots // n
    slow, fast = factors(n)
    chunks, half = CHUNKS, CHUNKS // 2
    dc = width // chunks
    peers = max(fast - 1, 1)
    dma = pltpu.SemaphoreType.DMA
    vm = pltpu.VMEM
    scratch = [
        vm(routes.shape, jnp.int32),
        vm((tokens, width), BF16),
        vm((chunks, dc, hidden), BF16),
        vm((slots, hidden), BF16),
        vm((chunks, cap, dc), BF16),
        vm((chunks, n, cap, dc), BF16),
        vm((chunks, slots, dc), BF16),
        vm((slots, hidden), F32),
        vm((slots, hidden), BF16),
        vm((chunks, n, cap, dc), F32),
        vm((chunks, fast, slow, cap, dc), BF16),
        vm((chunks, peers, slow, cap, dc), BF16),
        vm((chunks, slow, cap, dc), BF16),
        vm((chunks, slow, cap, dc), BF16),
        vm((chunks, slow, cap, dc), BF16),
        vm((cap, dc), F32),
        vm((chunks, cap, dc), BF16),
        vm((chunks, cap, dc), BF16),
        vm((chunks, tokens, dc), BF16),
        vm((half, dc, hidden), BF16),
        vm((half, dc, hidden), BF16),
        vm((half, dc, hidden), BF16),
        dma((2 + chunks,)),
        dma((2,)),
        dma((chunks,)),
        dma((chunks, n)),
        dma((chunks, slow, 1 + fast)),
        dma((chunks, peers)),
        dma((chunks, peers)),
        dma((chunks, slow)),
        dma((2, chunks, slow)),
        dma((chunks,)),
        dma((chunks,)),
        dma((half,)),
        dma((half,)),
        dma((chunks + half,)),
    ]
    anywhere = pl.BlockSpec(memory_space=pl.ANY)
    weight_grad, acts_grad = pl.pallas_call(
        functools.partial(kernel, n, pipe, cap),
        out_shape=(
            jax.ShapeDtypeStruct((width // 2, hidden), BF16),
            jax.ShapeDtypeStruct((tokens, width), BF16),
        ),
        in_specs=[anywhere] * 4,
        out_specs=(anywhere, anywhere),
        scratch_shapes=scratch,
        compiler_params=pltpu.CompilerParams(
            collective_id=0, has_side_effects=True, vmem_limit_bytes=56 * 1024 * 1024
        ),
        cost_estimate=pl.CostEstimate(
            flops=6 * slots * width * hidden,
            bytes_accessed=3 * width * hidden + 4 * tokens * width,
            transcendentals=slots * hidden,
        ),
    )(routes, acts, weight, cot)
    return (weight_grad[None], acts_grad[None, None])


def solution(mesh):
    return jax.shard_map(
        per_device,
        mesh=mesh,
        in_specs=(
            P("pipe", "rep", "fsdp", None),
            P("pipe", "rep", "fsdp", None),
            P("pipe", None, "fsdp"),
            P("pipe", "rep", None, "fsdp"),
        ),
        out_specs=(P("pipe", "rep", "fsdp"), P("pipe", "rep", "fsdp", None)),
        check_vma=False,
    )
```

```python
import functools

import jax
import jax.numpy as jnp
from jax import lax
from jax.experimental import pallas as pl
from jax.experimental.pallas import tpu as pltpu
from jax.sharding import PartitionSpec as P

MESH = pl.DeviceIdType.MESH
F32 = jnp.float32
BF16 = jnp.bfloat16
CHUNKS = 4


def factors(n):
    fast = 1
    while (fast * 2) ** 2 <= n:
        fast *= 2
    return n // fast, fast


def kernel(
    n, pipe, cap,
    routes_hbm, acts_hbm, weight_hbm, cot_hbm,
    w_sum, spread,
    ids, acts, weight, cot, compacted, gathered, rows, acc, pre_grad,
    own_term, y_out, y_in, z_out, up_in, down_in, total, done, back,
    w_out, w_in,
    local_sem, ids_sem, x_send, g_recv, g_send, y_send, y_recv, z_send, z_recv,
    b_send, b_recv, w_send, w_recv,
):
    chunks = CHUNKS
    slow, fast = factors(n)
    p, f, r = lax.axis_index("pipe"), lax.axis_index("fsdp"), lax.axis_index("rep")
    a, b = f // fast, lax.rem(f, fast)
    nxt, prv = lax.rem(p + 1, pipe), lax.rem(p + pipe - 1, pipe)
    slots = n * cap
    dc = weight.shape[1]
    half = chunks // 2
    has_up, has_down = a < slow - 1, a > 0
    up, down = (a + 1) * fast + b, (a - 1) * fast + b

    def peer(j):
        return a * fast + lax.rem(b + j, fast)

    def remote(src, dst, send, recv, where):
        return pltpu.make_async_remote_copy(
            src_ref=src, dst_ref=dst, send_sem=send, recv_sem=recv,
            device_id=where, device_id_type=MESH,
        )

    def greet(where):
        pl.semaphore_signal(barrier, inc=1, device_id=where, device_id_type=MESH)

    acts_load = pltpu.make_async_copy(acts_hbm, acts, local_sem.at[0])
    acts_load.start()
    barrier = pltpu.get_barrier_semaphore()
    greet({"pipe": prv})
    if pipe > 2:
        greet({"pipe": nxt})
    greet({"rep": 1 - r})
    for j in range(1, fast):
        greet({"fsdp": peer(j)})

    @pl.when(has_up)
    def _():
        greet({"fsdp": up})

    @pl.when(has_down)
    def _():
        greet({"fsdp": down})

    weight_loads = []
    for c in range(chunks):
        load = pltpu.make_async_copy(
            weight_hbm.at[pl.ds(c * dc, dc)], weight.at[c], local_sem.at[2 + c]
        )
        load.start()
        weight_loads.append(load)
    cot_load = pltpu.make_async_copy(cot_hbm, cot, local_sem.at[1])
    cot_load.start()

    greeted = (1 if pipe == 2 else 2) + 1 + (fast - 1)
    pl.semaphore_wait(
        barrier, greeted + has_up.astype(jnp.int32) + has_down.astype(jnp.int32)
    )

    ids_copy = remote(routes_hbm, ids, ids_sem.at[0], ids_sem.at[1], {"pipe": prv})
    ids_copy.start()
    ids_copy.wait_recv()
    tokens = ids.shape[1]
    named = jnp.where(ids[...] == 0, 1.0, 0.0).astype(F32)
    chosen = jnp.max(named, axis=0, keepdims=True)
    row = lax.broadcasted_iota(jnp.int32, (tokens, tokens), 0)
    col = lax.broadcasted_iota(jnp.int32, (tokens, tokens), 1)
    before = jnp.where(row <= col, 1.0, 0.0).astype(BF16)
    chosen8 = jnp.broadcast_to(chosen, (16, tokens))
    ordinal = jnp.dot(chosen8.astype(BF16), before, preferred_element_type=F32)[0:1] - 1.0
    hits = jnp.where(
        (jnp.broadcast_to(ordinal, (tokens, tokens)) == row.astype(F32))
        & (jnp.broadcast_to(chosen, (tokens, tokens)) > 0.5),
        1.0, 0.0,
    ).astype(F32)
    picker = hits[0:cap].astype(BF16)
    spreader = hits.T.astype(BF16)
    acts_load.wait()

    def x_copy(c):
        return remote(
            compacted.at[c], gathered.at[c, f], x_send.at[c], g_recv.at[c, f], {"pipe": nxt}
        )

    for c in range(chunks):
        compacted[c] = jnp.dot(
            picker, acts[:, c * dc:(c + 1) * dc], preferred_element_type=F32
        ).astype(BF16)
        x_copy(c).start()

    def g_copy(c, origin, kind, where):
        block = origin * fast + b
        return remote(
            gathered.at[c, block], gathered.at[c, block],
            g_send.at[c, origin, kind], g_recv.at[c, block], {"fsdp": where},
        )

    def g_wait(c, block):
        remote(
            gathered.at[c, block], gathered.at[c, block],
            g_send.at[c, 0, 0], g_recv.at[c, block], {"pipe": nxt},
        ).wait_recv()

    def g_fan(c, origin, act):
        for j in range(1, fast):
            act(g_copy(c, origin, 1 + j, peer(j)))

    def g_step(c, k, act, wait):
        if k == 0:
            if wait:
                g_wait(c, f)

            @pl.when(has_up)
            def _():
                act(g_copy(c, a, 0, up))

            @pl.when(has_down)
            def _():
                act(g_copy(c, a, 1, down))

            g_fan(c, a, act)
            return

        @pl.when(a - k >= 0)
        def _():
            if wait:
                g_wait(c, (a - k) * fast + b)

            @pl.when(has_up)
            def _():
                act(g_copy(c, a - k, 0, up))

            g_fan(c, a - k, act)

        @pl.when(a + k < slow)
        def _():
            if wait:
                g_wait(c, (a + k) * fast + b)

            @pl.when(has_down)
            def _():
                act(g_copy(c, a + k, 1, down))

            g_fan(c, a + k, act)

    def first_matmul(c):
        for origin in range(slow):
            for j in range(1, fast):
                g_wait(c, origin * fast + lax.rem(b + j, fast))
        block = gathered[c].astype(F32).reshape(slots, dc).astype(BF16)
        rows[c] = block
        weight_loads[c].wait()
        part = jnp.dot(block, weight[c], preferred_element_type=F32)
        if c == 0:
            acc[...] = part
        else:
            acc[...] += part

    steps = sorted((c + 2 * k, k, c) for c in range(chunks) for k in range(slow))
    for _, k, c in steps:
        g_step(c, k, lambda copy: copy.start(), True)
        if k == slow - 1:
            first_matmul(c)

    cot_load.wait()
    piece = 48
    for i in range(slots // piece):
        span = pl.ds(i * piece, piece)
        pre = acc[span]
        s = jax.nn.sigmoid(pre)
        pre_grad[span] = (cot[span].astype(F32) * s * (1.0 + pre * (1.0 - s))).astype(BF16)

    def y_copy(c, j, dest):
        to = lax.rem(b + j, fast)
        return remote(
            y_out.at[c, to, dest], y_in.at[c, j - 1, dest], y_send.at[c, j - 1, dest],
            y_recv.at[c, j - 1, dest], {"fsdp": peer(j)},
        )

    def slot_matmul(c):
        term = lax.dot_general(
            pre_grad[...], weight[c], (((1,), (1,)), ((), ())), preferred_element_type=F32
        ).reshape(n, cap, dc)
        own_term[c] = term
        for aa in range(slow):
            for bb in range(fast):
                y_out[c, bb, aa] = term[aa * fast + bb].astype(BF16)
        far_first = sorted(range(slow), key=lambda dest: -abs(2 * dest - slow + 1))
        for dest in far_first:
            for j in range(1, fast):
                y_copy(c, j, dest).start()

    def partial(c, dest):
        value = own_term[c, dest * fast + b]
        for j in range(1, fast):
            y_copy(c, j, dest).wait_recv()
            value = value + y_in[c, j - 1, dest].astype(F32)
        return value

    def z_copy(c, dest, way):
        landing = up_in if way == 0 else down_in
        return remote(
            z_out.at[c, dest], landing.at[c, dest], z_send.at[c, dest],
            z_recv.at[way, c, dest], {"fsdp": up if way == 0 else down},
        )

    def z_wait(c, dest, way):
        z_copy(c, dest, way).wait_recv()

    def line(c, dest, way):
        landing = up_in if way == 0 else down_in
        middle = has_down if way == 0 else has_up

        @pl.when(middle)
        def _():
            z_wait(c, dest, way)
            z_out[c, dest] = (partial(c, dest) + landing[c, dest].astype(F32)).astype(BF16)

        @pl.when(jnp.logical_not(middle))
        def _():
            z_out[c, dest] = partial(c, dest).astype(BF16)

        z_copy(c, dest, way).start()

    def back_copy(c):
        return remote(done.at[c], back.at[c], b_send.at[c], b_recv.at[c], {"pipe": prv})

    def r_step(c, k):
        if k < slow - 1:
            top, bottom = slow - 1 - k, k

            @pl.when(top > a)
            def _():
                line(c, top, 0)

            @pl.when(bottom < a)
            def _():
                line(c, bottom, 1)

            return
        total[...] = partial(c, a)

        @pl.when(has_down)
        def _():
            z_wait(c, a, 0)
            total[...] += up_in[c, a].astype(F32)

        @pl.when(has_up)
        def _():
            z_wait(c, a, 1)
            total[...] += down_in[c, a].astype(F32)

        done[c] = total[...].astype(BF16)
        back_copy(c).start()

    def weight_tile(index):
        return lax.dot_general(
            rows[index], pre_grad[...], (((0,), (0,)), ((), ())), preferred_element_type=F32
        ).astype(BF16)

    def w_copy(i):
        return remote(w_out.at[i], w_in.at[i], w_send.at[i], w_recv.at[i], {"rep": 1 - r})

    def other_half(i):
        w_out[i] = weight_tile((1 - r) * half + i)
        w_copy(i).start()

    def own_half(i):
        w_sum[i] = weight_tile(r * half + i)

    def add_halves(i):
        w_copy(i).wait_recv()
        w_sum[i] = (w_sum[i].astype(F32) + w_in[i].astype(F32)).astype(BF16)

    def put_back(c):
        back_copy(c).wait_recv()
        grads = back[c].astype(F32)
        padded = jnp.concatenate(
            [grads, jnp.zeros((tokens - cap, dc), F32)], axis=0
        ).astype(BF16)
        spread[:, c * dc:(c + 1) * dc] = jnp.dot(
            spreader, padded, preferred_element_type=F32
        ).astype(BF16)

    beside = [functools.partial(other_half, i) for i in range(half)]
    beside += [functools.partial(own_half, i) for i in range(half)]
    for t in range(-2, chunks + slow - 1):
        if 0 <= t + 2 < chunks:
            slot_matmul(t + 2)
        for c in range(chunks):
            if 0 <= t - c < slow:
                r_step(c, t - c)
        if beside:
            beside.pop(0)()
    for c in range(chunks - 1):
        put_back(c)
    for i in range(half):
        add_halves(i)
    put_back(chunks - 1)

    ids_copy.wait_send()
    for c in range(chunks):
        x_copy(c).wait_send()
        for k in range(slow):
            g_step(c, k, lambda copy: copy.wait_send(), False)
        for dest in range(slow):
            for j in range(1, fast):
                y_copy(c, j, dest).wait_send()

            @pl.when(dest != a)
            def _():
                z_copy(c, dest, 0).wait_send()

        back_copy(c).wait_send()
    for i in range(half):
        w_copy(i).wait_send()


def per_device(section_acts, route_ids, gate_weight, hidden_cot):
    n, pipe = lax.axis_size("fsdp"), lax.axis_size("pipe")
    acts, weight, cot = section_acts[0, 0], gate_weight[0], hidden_cot[0, 0]
    routes = route_ids[0, 0].T
    tokens, width = acts.shape
    slots, hidden = cot.shape
    cap = slots // n
    slow, fast = factors(n)
    chunks, half = CHUNKS, CHUNKS // 2
    dc = width // chunks
    peers = max(fast - 1, 1)
    dma = pltpu.SemaphoreType.DMA
    vm = pltpu.VMEM
    scratch = [
        vm(routes.shape, jnp.int32),
        vm((tokens, width), BF16),
        vm((chunks, dc, hidden), BF16),
        vm((slots, hidden), BF16),
        vm((chunks, cap, dc), BF16),
        vm((chunks, n, cap, dc), BF16),
        vm((chunks, slots, dc), BF16),
        vm((slots, hidden), F32),
        vm((slots, hidden), BF16),
        vm((chunks, n, cap, dc), F32),
        vm((chunks, fast, slow, cap, dc), BF16),
        vm((chunks, peers, slow, cap, dc), BF16),
        vm((chunks, slow, cap, dc), BF16),
        vm((chunks, slow, cap, dc), BF16),
        vm((chunks, slow, cap, dc), BF16),
        vm((cap, dc), F32),
        vm((chunks, cap, dc), BF16),
        vm((chunks, cap, dc), BF16),
        vm((half, dc, hidden), BF16),
        vm((half, dc, hidden), BF16),
        dma((2 + chunks,)),
        dma((2,)),
        dma((chunks,)),
        dma((chunks, n)),
        dma((chunks, slow, 1 + fast)),
        dma((chunks, peers, slow)),
        dma((chunks, peers, slow)),
        dma((chunks, slow)),
        dma((2, chunks, slow)),
        dma((chunks,)),
        dma((chunks,)),
        dma((half,)),
        dma((half,)),
    ]
    anywhere = pl.BlockSpec(memory_space=pl.ANY)
    inside = pl.BlockSpec(memory_space=pltpu.VMEM)
    weight_grad, acts_grad = pl.pallas_call(
        functools.partial(kernel, n, pipe, cap),
        out_shape=(
            vm((half, dc, hidden), BF16),
            vm((tokens, width), BF16),
        ),
        in_specs=[anywhere] * 4,
        out_specs=(inside, inside),
        scratch_shapes=scratch,
        compiler_params=pltpu.CompilerParams(
            collective_id=0, has_side_effects=True, vmem_limit_bytes=56 * 1024 * 1024
        ),
        cost_estimate=pl.CostEstimate(
            flops=6 * slots * width * hidden,
            bytes_accessed=3 * width * hidden + 4 * tokens * width,
            transcendentals=slots * hidden,
        ),
    )(routes, acts, weight, cot)
    return (weight_grad.reshape(1, width // 2, hidden), acts_grad[None, None])


def solution(mesh):
    return jax.shard_map(
        per_device,
        mesh=mesh,
        in_specs=(
            P("pipe", "rep", "fsdp", None),
            P("pipe", "rep", "fsdp", None),
            P("pipe", None, "fsdp"),
            P("pipe", "rep", None, "fsdp"),
        ),
        out_specs=(P("pipe", "rep", "fsdp"), P("pipe", "rep", "fsdp", None)),
        check_vma=False,
    )
```

```python
import functools

import jax
import jax.numpy as jnp
from jax import lax
from jax.experimental import pallas as pl
from jax.experimental.pallas import tpu as pltpu
from jax.sharding import PartitionSpec as P

MESH = pl.DeviceIdType.MESH
F32 = jnp.float32
BF16 = jnp.bfloat16
CHUNKS = 4


def factors(n):
    fast = 1
    while (fast * 2) ** 2 <= n:
        fast *= 2
    return n // fast, fast


def kernel(
    n, pipe, cap,
    routes_hbm, acts_hbm, weight_hbm, cot_hbm,
    w_sum, spread,
    ids, acts, weight, cot, compacted, gathered, rows, rows_out, acc, pre_grad,
    own_term, y_out, y_in, z_out, up_in, down_in, total, done, back,
    local_sem, ids_sem, x_send, g_recv, g_send, y_send, y_recv, z_send, z_recv,
    b_send, b_recv, f_send, f_recv,
):
    chunks = CHUNKS
    slow, fast = factors(n)
    p, f, r = lax.axis_index("pipe"), lax.axis_index("fsdp"), lax.axis_index("rep")
    a, b = f // fast, lax.rem(f, fast)
    nxt, prv = lax.rem(p + 1, pipe), lax.rem(p + pipe - 1, pipe)
    slots = n * cap
    dc = weight.shape[1]
    half = chunks // 2
    has_up, has_down = a < slow - 1, a > 0
    up, down = (a + 1) * fast + b, (a - 1) * fast + b

    def peer(j):
        return a * fast + lax.rem(b + j, fast)

    def remote(src, dst, send, recv, where):
        return pltpu.make_async_remote_copy(
            src_ref=src, dst_ref=dst, send_sem=send, recv_sem=recv,
            device_id=where, device_id_type=MESH,
        )

    def greet(where):
        pl.semaphore_signal(barrier, inc=1, device_id=where, device_id_type=MESH)

    acts_load = pltpu.make_async_copy(acts_hbm, acts, local_sem.at[0])
    acts_load.start()
    barrier = pltpu.get_barrier_semaphore()
    greet({"pipe": prv})
    if pipe > 2:
        greet({"pipe": nxt})
    greet({"rep": 1 - r})
    for j in range(1, fast):
        greet({"fsdp": peer(j)})

    @pl.when(has_up)
    def _():
        greet({"fsdp": up})

    @pl.when(has_down)
    def _():
        greet({"fsdp": down})

    weight_loads = []
    for c in range(chunks):
        load = pltpu.make_async_copy(
            weight_hbm.at[pl.ds(c * dc, dc)], weight.at[c], local_sem.at[2 + c]
        )
        load.start()
        weight_loads.append(load)
    cot_load = pltpu.make_async_copy(cot_hbm, cot, local_sem.at[1])
    cot_load.start()

    greeted = (1 if pipe == 2 else 2) + 1 + (fast - 1)
    pl.semaphore_wait(
        barrier, greeted + has_up.astype(jnp.int32) + has_down.astype(jnp.int32)
    )

    ids_copy = remote(routes_hbm, ids, ids_sem.at[0], ids_sem.at[1], {"pipe": prv})
    ids_copy.start()
    ids_copy.wait_recv()
    tokens = ids.shape[1]
    named = jnp.where(ids[...] == 0, 1.0, 0.0).astype(F32)
    chosen = jnp.max(named, axis=0, keepdims=True)
    row = lax.broadcasted_iota(jnp.int32, (tokens, tokens), 0)
    col = lax.broadcasted_iota(jnp.int32, (tokens, tokens), 1)
    before = jnp.where(row <= col, 1.0, 0.0).astype(BF16)
    chosen8 = jnp.broadcast_to(chosen, (16, tokens))
    ordinal = jnp.dot(chosen8.astype(BF16), before, preferred_element_type=F32)[0:1] - 1.0
    hits = jnp.where(
        (jnp.broadcast_to(ordinal, (tokens, tokens)) == row.astype(F32))
        & (jnp.broadcast_to(chosen, (tokens, tokens)) > 0.5),
        1.0, 0.0,
    ).astype(F32)
    picker = hits[0:cap].astype(BF16)
    spreader = hits.T.astype(BF16)
    acts_load.wait()

    def x_copy(c):
        return remote(
            compacted.at[c], gathered.at[c, f], x_send.at[c], g_recv.at[c, f], {"pipe": nxt}
        )

    for c in range(chunks):
        compacted[c] = jnp.dot(
            picker, acts[:, c * dc:(c + 1) * dc], preferred_element_type=F32
        ).astype(BF16)
        x_copy(c).start()

    def g_copy(c, origin, kind, where):
        block = origin * fast + b
        return remote(
            gathered.at[c, block], gathered.at[c, block],
            g_send.at[c, origin, kind], g_recv.at[c, block], {"fsdp": where},
        )

    def g_wait(c, block):
        remote(
            gathered.at[c, block], gathered.at[c, block],
            g_send.at[c, 0, 0], g_recv.at[c, block], {"pipe": nxt},
        ).wait_recv()

    def g_fan(c, origin, act):
        for j in range(1, fast):
            act(g_copy(c, origin, 1 + j, peer(j)))

    def g_step(c, k, act, wait):
        if k == 0:
            if wait:
                g_wait(c, f)

            @pl.when(has_up)
            def _():
                act(g_copy(c, a, 0, up))

            @pl.when(has_down)
            def _():
                act(g_copy(c, a, 1, down))

            g_fan(c, a, act)
            return

        @pl.when(a - k >= 0)
        def _():
            if wait:
                g_wait(c, (a - k) * fast + b)

            @pl.when(has_up)
            def _():
                act(g_copy(c, a - k, 0, up))

            g_fan(c, a - k, act)

        @pl.when(a + k < slow)
        def _():
            if wait:
                g_wait(c, (a + k) * fast + b)

            @pl.when(has_down)
            def _():
                act(g_copy(c, a + k, 1, down))

            g_fan(c, a + k, act)

    def rows_copy(i):
        return remote(rows_out.at[i], rows.at[i, 1], f_send.at[i], f_recv.at[i], {"rep": 1 - r})

    grad_copy = remote(
        pre_grad.at[0], pre_grad.at[1], f_send.at[half], f_recv.at[half], {"rep": 1 - r}
    )

    def first_matmul(c):
        for origin in range(slow):
            for j in range(1, fast):
                g_wait(c, origin * fast + lax.rem(b + j, fast))
        block = gathered[c].astype(F32).reshape(slots, dc).astype(BF16)
        i, mine = c % half, r == c // half

        @pl.when(mine)
        def _():
            rows[i, 0] = block

        @pl.when(jnp.logical_not(mine))
        def _():
            rows_out[i] = block
            rows_copy(i).start()

        weight_loads[c].wait()
        part = jnp.dot(block, weight[c], preferred_element_type=F32)
        if c == 0:
            acc[...] = part
        else:
            acc[...] += part

    steps = sorted((c + 2 * k, k, c) for c in range(chunks) for k in range(slow))
    for _, k, c in steps:
        g_step(c, k, lambda copy: copy.start(), True)
        if k == slow - 1:
            first_matmul(c)

    cot_load.wait()
    piece = 48
    for i in range(slots // piece):
        span = pl.ds(i * piece, piece)
        pre = acc[span]
        s = jax.nn.sigmoid(pre)
        pre_grad[0, span] = (cot[span].astype(F32) * s * (1.0 + pre * (1.0 - s))).astype(BF16)
    grad_copy.start()

    def y_copy(c, j, dest):
        to = lax.rem(b + j, fast)
        return remote(
            y_out.at[c, to, dest], y_in.at[c, j - 1, dest], y_send.at[c, j - 1, dest],
            y_recv.at[c, j - 1, dest], {"fsdp": peer(j)},
        )

    def slot_matmul(c):
        term = lax.dot_general(
            pre_grad[0], weight[c], (((1,), (1,)), ((), ())), preferred_element_type=F32
        ).reshape(n, cap, dc)
        own_term[c] = term
        for aa in range(slow):
            for bb in range(fast):
                y_out[c, bb, aa] = term[aa * fast + bb].astype(BF16)
        far_first = sorted(range(slow), key=lambda dest: -abs(2 * dest - slow + 1))
        for dest in far_first:
            for j in range(1, fast):
                y_copy(c, j, dest).start()

    def partial(c, dest):
        value = own_term[c, dest * fast + b]
        for j in range(1, fast):
            y_copy(c, j, dest).wait_recv()
            value = value + y_in[c, j - 1, dest].astype(F32)
        return value

    def z_copy(c, dest, way):
        landing = up_in if way == 0 else down_in
        return remote(
            z_out.at[c, dest], landing.at[c, dest], z_send.at[c, dest],
            z_recv.at[way, c, dest], {"fsdp": up if way == 0 else down},
        )

    def z_wait(c, dest, way):
        z_copy(c, dest, way).wait_recv()

    def line(c, dest, way):
        landing = up_in if way == 0 else down_in
        middle = has_down if way == 0 else has_up

        @pl.when(middle)
        def _():
            z_wait(c, dest, way)
            z_out[c, dest] = (partial(c, dest) + landing[c, dest].astype(F32)).astype(BF16)

        @pl.when(jnp.logical_not(middle))
        def _():
            z_out[c, dest] = partial(c, dest).astype(BF16)

        z_copy(c, dest, way).start()

    def back_copy(c):
        return remote(done.at[c], back.at[c], b_send.at[c], b_recv.at[c], {"pipe": prv})

    def r_step(c, k):
        if k < slow - 1:
            top, bottom = slow - 1 - k, k

            @pl.when(top > a)
            def _():
                line(c, top, 0)

            @pl.when(bottom < a)
            def _():
                line(c, bottom, 1)

            return
        total[...] = partial(c, a)

        @pl.when(has_down)
        def _():
            z_wait(c, a, 0)
            total[...] += up_in[c, a].astype(F32)

        @pl.when(has_up)
        def _():
            z_wait(c, a, 1)
            total[...] += down_in[c, a].astype(F32)

        done[c] = total[...].astype(BF16)
        back_copy(c).start()

    def weight_tile(i):
        if i == 0:
            grad_copy.wait_recv()
        rows_copy(i).wait_recv()
        w_sum[i] = lax.dot_general(
            rows[i].reshape(2 * slots, dc), pre_grad[...].reshape(2 * slots, -1),
            (((0,), (0,)), ((), ())), preferred_element_type=F32,
        ).astype(BF16)

    def put_back(c):
        back_copy(c).wait_recv()
        grads = back[c].astype(F32)
        padded = jnp.concatenate(
            [grads, jnp.zeros((tokens - cap, dc), F32)], axis=0
        ).astype(BF16)
        spread[:, c * dc:(c + 1) * dc] = jnp.dot(
            spreader, padded, preferred_element_type=F32
        ).astype(BF16)

    beside = [functools.partial(weight_tile, i) for i in range(half)]
    for t in range(-2, chunks + slow - 1):
        if 0 <= t + 2 < chunks:
            slot_matmul(t + 2)
        for c in range(chunks):
            if 0 <= t - c < slow:
                r_step(c, t - c)
        if t >= 0 and beside:
            beside.pop(0)()
    for c in range(chunks):
        put_back(c)

    ids_copy.wait_send()
    for c in range(chunks):
        x_copy(c).wait_send()
        for k in range(slow):
            g_step(c, k, lambda copy: copy.wait_send(), False)
        for dest in range(slow):
            for j in range(1, fast):
                y_copy(c, j, dest).wait_send()

            @pl.when(dest != a)
            def _():
                z_copy(c, dest, 0).wait_send()

        back_copy(c).wait_send()
    for i in range(half):
        rows_copy(i).wait_send()
    grad_copy.wait_send()


def per_device(section_acts, route_ids, gate_weight, hidden_cot):
    n, pipe = lax.axis_size("fsdp"), lax.axis_size("pipe")
    acts, weight, cot = section_acts[0, 0], gate_weight[0], hidden_cot[0, 0]
    routes = route_ids[0, 0].T
    tokens, width = acts.shape
    slots, hidden = cot.shape
    cap = slots // n
    slow, fast = factors(n)
    chunks, half = CHUNKS, CHUNKS // 2
    dc = width // chunks
    peers = max(fast - 1, 1)
    dma = pltpu.SemaphoreType.DMA
    vm = pltpu.VMEM
    scratch = [
        vm(routes.shape, jnp.int32),
        vm((tokens, width), BF16),
        vm((chunks, dc, hidden), BF16),
        vm((slots, hidden), BF16),
        vm((chunks, cap, dc), BF16),
        vm((chunks, n, cap, dc), BF16),
        vm((half, 2, slots, dc), BF16),
        vm((half, slots, dc), BF16),
        vm((slots, hidden), F32),
        vm((2, slots, hidden), BF16),
        vm((chunks, n, cap, dc), F32),
        vm((chunks, fast, slow, cap, dc), BF16),
        vm((chunks, peers, slow, cap, dc), BF16),
        vm((chunks, slow, cap, dc), BF16),
        vm((chunks, slow, cap, dc), BF16),
        vm((chunks, slow, cap, dc), BF16),
        vm((cap, dc), F32),
        vm((chunks, cap, dc), BF16),
        vm((chunks, cap, dc), BF16),
        dma((2 + chunks,)),
        dma((2,)),
        dma((chunks,)),
        dma((chunks, n)),
        dma((chunks, slow, 1 + fast)),
        dma((chunks, peers, slow)),
        dma((chunks, peers, slow)),
        dma((chunks, slow)),
        dma((2, chunks, slow)),
        dma((chunks,)),
        dma((chunks,)),
        dma((half + 1,)),
        dma((half + 1,)),
    ]
    anywhere = pl.BlockSpec(memory_space=pl.ANY)
    inside = pl.BlockSpec(memory_space=pltpu.VMEM)
    weight_grad, acts_grad = pl.pallas_call(
        functools.partial(kernel, n, pipe, cap),
        out_shape=(
            vm((half, dc, hidden), BF16),
            vm((tokens, width), BF16),
        ),
        in_specs=[anywhere] * 4,
        out_specs=(inside, inside),
        scratch_shapes=scratch,
        compiler_params=pltpu.CompilerParams(
            collective_id=0, has_side_effects=True, vmem_limit_bytes=56 * 1024 * 1024
        ),
        cost_estimate=pl.CostEstimate(
            flops=6 * slots * width * hidden,
            bytes_accessed=3 * width * hidden + 4 * tokens * width,
            transcendentals=slots * hidden,
        ),
    )(routes, acts, weight, cot)
    return (weight_grad.reshape(1, width // 2, hidden), acts_grad[None, None])


def solution(mesh):
    return jax.shard_map(
        per_device,
        mesh=mesh,
        in_specs=(
            P("pipe", "rep", "fsdp", None),
            P("pipe", "rep", "fsdp", None),
            P("pipe", None, "fsdp"),
            P("pipe", "rep", None, "fsdp"),
        ),
        out_specs=(P("pipe", "rep", "fsdp"), P("pipe", "rep", "fsdp", None)),
        check_vma=False,
    )
```

```python
import functools

import jax
import jax.numpy as jnp
from jax import lax
from jax.experimental import pallas as pl
from jax.experimental.pallas import tpu as pltpu
from jax.sharding import PartitionSpec as P

MESH = pl.DeviceIdType.MESH
F32 = jnp.float32
BF16 = jnp.bfloat16
CHUNKS = 4


def factors(n):
    fast = 1
    while (fast * 2) ** 2 <= n:
        fast *= 2
    return n // fast, fast


def kernel(
    n, pipe, cap,
    routes_hbm, acts_hbm, weight_hbm, cot_hbm,
    w_sum, spread,
    ids, acts, weight, cot, compacted, gathered, rows, rows_out, acc, pre_grad,
    own_term, y_out, y_in, z_out, z_in, done, back,
    local_sem, ids_sem, x_send, g_recv, gs_send, gf_send, y_send, y_recv, z_send, z_recv,
    b_send, b_recv, f_send, f_recv,
):
    chunks = CHUNKS
    slow, fast = factors(n)
    p, f, r = lax.axis_index("pipe"), lax.axis_index("fsdp"), lax.axis_index("rep")
    a, b = f // fast, lax.rem(f, fast)
    nxt, prv = lax.rem(p + 1, pipe), lax.rem(p + pipe - 1, pipe)
    slots = n * cap
    dc = weight.shape[1]
    half = chunks // 2

    def peer(j):
        return a * fast + lax.rem(b + j, fast)

    def ahead(k):
        return lax.rem(a + k, slow)

    def behind(k):
        return lax.rem(a + slow - k, slow)

    def remote(src, dst, send, recv, where):
        return pltpu.make_async_remote_copy(
            src_ref=src, dst_ref=dst, send_sem=send, recv_sem=recv,
            device_id=where, device_id_type=MESH,
        )

    def greet(where):
        pl.semaphore_signal(barrier, inc=1, device_id=where, device_id_type=MESH)

    acts_load = pltpu.make_async_copy(acts_hbm, acts, local_sem.at[0])
    acts_load.start()
    barrier = pltpu.get_barrier_semaphore()
    greet({"pipe": prv})
    if pipe > 2:
        greet({"pipe": nxt})
    greet({"rep": 1 - r})
    for j in range(1, fast):
        greet({"fsdp": peer(j)})

    for k in range(1, slow):
        greet({"fsdp": ahead(k) * fast + b})

    weight_loads = []
    for c in range(chunks):
        load = pltpu.make_async_copy(
            weight_hbm.at[pl.ds(c * dc, dc)], weight.at[c], local_sem.at[2 + c]
        )
        load.start()
        weight_loads.append(load)
    cot_load = pltpu.make_async_copy(cot_hbm, cot, local_sem.at[1])
    cot_load.start()

    pl.semaphore_wait(barrier, (1 if pipe == 2 else 2) + 1 + (fast - 1) + (slow - 1))

    ids_copy = remote(routes_hbm, ids, ids_sem.at[0], ids_sem.at[1], {"pipe": prv})
    ids_copy.start()
    ids_copy.wait_recv()
    tokens = ids.shape[1]
    named = jnp.where(ids[...] == 0, 1.0, 0.0).astype(F32)
    chosen = jnp.max(named, axis=0, keepdims=True)
    row = lax.broadcasted_iota(jnp.int32, (tokens, tokens), 0)
    col = lax.broadcasted_iota(jnp.int32, (tokens, tokens), 1)
    before = jnp.where(row <= col, 1.0, 0.0).astype(BF16)
    chosen8 = jnp.broadcast_to(chosen, (16, tokens))
    ordinal = jnp.dot(chosen8.astype(BF16), before, preferred_element_type=F32)[0:1] - 1.0
    hits = jnp.where(
        (jnp.broadcast_to(ordinal, (tokens, tokens)) == row.astype(F32))
        & (jnp.broadcast_to(chosen, (tokens, tokens)) > 0.5),
        1.0, 0.0,
    ).astype(F32)
    picker = hits[0:cap].astype(BF16)
    spreader = hits.T.astype(BF16)
    acts_load.wait()

    def x_copy(c):
        return remote(
            compacted.at[c], gathered.at[c, f], x_send.at[c], g_recv.at[c, f], {"pipe": nxt}
        )

    for c in range(chunks):
        compacted[c] = jnp.dot(
            picker, acts[:, c * dc:(c + 1) * dc], preferred_element_type=F32
        ).astype(BF16)
        x_copy(c).start()

    def g_wait(c, block):
        remote(
            gathered.at[c, block], gathered.at[c, block],
            gs_send.at[c, 0], g_recv.at[c, block], {"pipe": nxt},
        ).wait_recv()

    def slow_copy(c, k):
        return remote(
            gathered.at[c, f], gathered.at[c, f], gs_send.at[c, k - 1], g_recv.at[c, f],
            {"fsdp": behind(k) * fast + b},
        )

    def fast_copy(c, k, j):
        block = ahead(k) * fast + b
        return remote(
            gathered.at[c, block], gathered.at[c, block], gf_send.at[c, k, j - 1],
            g_recv.at[c, block], {"fsdp": peer(j)},
        )

    def send_own(c):
        g_wait(c, f)
        for j in range(1, fast):
            fast_copy(c, 0, j).start()
        for k in range(1, slow):
            slow_copy(c, k).start()

    def pass_on(c):
        for k in range(1, slow):
            g_wait(c, ahead(k) * fast + b)
            for j in range(1, fast):
                fast_copy(c, k, j).start()

    def rows_copy(i):
        return remote(rows_out.at[i], rows.at[i, 1], f_send.at[i], f_recv.at[i], {"rep": 1 - r})

    grad_copy = remote(
        pre_grad.at[0], pre_grad.at[1], f_send.at[half], f_recv.at[half], {"rep": 1 - r}
    )

    def first_matmul(c):
        for k in range(slow):
            for j in range(1, fast):
                g_wait(c, ahead(k) * fast + lax.rem(b + j, fast))
        block = gathered[c].astype(F32).reshape(slots, dc).astype(BF16)
        i, mine = c % half, r == c // half

        @pl.when(mine)
        def _():
            rows[i, 0] = block

        @pl.when(jnp.logical_not(mine))
        def _():
            rows_out[i] = block
            rows_copy(i).start()

        weight_loads[c].wait()
        part = jnp.dot(block, weight[c], preferred_element_type=F32)
        if c == 0:
            acc[...] = part
        else:
            acc[...] += part

    for c in range(chunks):
        send_own(c)
    pass_on(0)
    for c in range(chunks):
        if c + 1 < chunks:
            pass_on(c + 1)
        first_matmul(c)

    cot_load.wait()
    piece = 48
    for i in range(slots // piece):
        span = pl.ds(i * piece, piece)
        pre = acc[span]
        s = jax.nn.sigmoid(pre)
        pre_grad[0, span] = (cot[span].astype(F32) * s * (1.0 + pre * (1.0 - s))).astype(BF16)
    grad_copy.start()

    def y_copy(c, j, k):
        to, dest = lax.rem(b + j, fast), behind(k)
        return remote(
            y_out.at[c, to, dest], y_in.at[c, j - 1, dest], y_send.at[c, j - 1, k],
            y_recv.at[c, j - 1, k], {"fsdp": peer(j)},
        )

    def slot_matmul(c):
        term = lax.dot_general(
            pre_grad[0], weight[c], (((1,), (1,)), ((), ())), preferred_element_type=F32
        ).reshape(n, cap, dc)
        own_term[c] = term
        for aa in range(slow):
            for bb in range(fast):
                y_out[c, bb, aa] = term[aa * fast + bb].astype(BF16)
        for k in [*range(1, slow), 0]:
            for j in range(1, fast):
                y_copy(c, j, k).start()

    def partial(c, k):
        dest = behind(k)
        value = own_term[c, dest * fast + b]
        for j in range(1, fast):
            y_copy(c, j, k).wait_recv()
            value = value + y_in[c, j - 1, dest].astype(F32)
        return value

    def z_copy(c, k):
        return remote(
            z_out.at[c, k - 1], z_in.at[c, k - 1], z_send.at[c, k - 1], z_recv.at[c, k - 1],
            {"fsdp": behind(k) * fast + b},
        )

    def send_partials(c):
        for k in range(1, slow):
            z_out[c, k - 1] = partial(c, k).astype(BF16)
            z_copy(c, k).start()

    def back_copy(c):
        return remote(done.at[c], back.at[c], b_send.at[c], b_recv.at[c], {"pipe": prv})

    def finish(c):
        total = partial(c, 0)
        for k in range(1, slow):
            z_copy(c, k).wait_recv()
            total = total + z_in[c, k - 1].astype(F32)
        done[c] = total.astype(BF16)
        back_copy(c).start()

    parts = 3
    depth = dc // parts

    def weight_tile(i, part):
        if part == 0:
            rows_copy(i).wait_recv()
            if i == 0:
                grad_copy.wait_recv()
        span = slice(part * depth, (part + 1) * depth)
        w_sum[i, span] = lax.dot_general(
            rows[i, :, :, span].reshape(2 * slots, depth), pre_grad[...].reshape(2 * slots, -1),
            (((0,), (0,)), ((), ())), preferred_element_type=F32,
        ).astype(BF16)

    def put_back(c):
        back_copy(c).wait_recv()
        grads = back[c].astype(F32)
        padded = jnp.concatenate(
            [grads, jnp.zeros((tokens - cap, dc), F32)], axis=0
        ).astype(BF16)
        spread[:, c * dc:(c + 1) * dc] = jnp.dot(
            spreader, padded, preferred_element_type=F32
        ).astype(BF16)

    beside = [functools.partial(weight_tile, i, j) for i in range(half) for j in range(parts)]
    beside.reverse()
    for c in range(chunks):
        slot_matmul(c)
        if c:
            send_partials(c - 1)
    beside.pop()()
    finish(0)
    send_partials(chunks - 1)
    for c in range(1, chunks):
        if beside:
            beside.pop()()
        finish(c)
    for c in range(chunks - 1):
        if beside:
            beside.pop()()
        put_back(c)
    while beside:
        beside.pop()()
    put_back(chunks - 1)

    ids_copy.wait_send()
    for c in range(chunks):
        x_copy(c).wait_send()
        for k in range(slow):
            for j in range(1, fast):
                fast_copy(c, k, j).wait_send()
                y_copy(c, j, k).wait_send()
            if k:
                slow_copy(c, k).wait_send()
                z_copy(c, k).wait_send()
        back_copy(c).wait_send()
    for i in range(half):
        rows_copy(i).wait_send()
    grad_copy.wait_send()


def per_device(section_acts, route_ids, gate_weight, hidden_cot):
    n, pipe = lax.axis_size("fsdp"), lax.axis_size("pipe")
    acts, weight, cot = section_acts[0, 0], gate_weight[0], hidden_cot[0, 0]
    routes = route_ids[0, 0].T
    tokens, width = acts.shape
    slots, hidden = cot.shape
    cap = slots // n
    slow, fast = factors(n)
    chunks, half = CHUNKS, CHUNKS // 2
    dc = width // chunks
    peers, hops = max(fast - 1, 1), max(slow - 1, 1)
    dma = pltpu.SemaphoreType.DMA
    vm = pltpu.VMEM
    scratch = [
        vm(routes.shape, jnp.int32),
        vm((tokens, width), BF16),
        vm((chunks, dc, hidden), BF16),
        vm((slots, hidden), BF16),
        vm((chunks, cap, dc), BF16),
        vm((chunks, n, cap, dc), BF16),
        vm((half, 2, slots, dc), BF16),
        vm((half, slots, dc), BF16),
        vm((slots, hidden), F32),
        vm((2, slots, hidden), BF16),
        vm((chunks, n, cap, dc), F32),
        vm((chunks, fast, slow, cap, dc), BF16),
        vm((chunks, peers, slow, cap, dc), BF16),
        vm((chunks, hops, cap, dc), BF16),
        vm((chunks, hops, cap, dc), BF16),
        vm((chunks, cap, dc), BF16),
        vm((chunks, cap, dc), BF16),
        dma((2 + chunks,)),
        dma((2,)),
        dma((chunks,)),
        dma((chunks, n)),
        dma((chunks, hops)),
        dma((chunks, slow, peers)),
        dma((chunks, peers, slow)),
        dma((chunks, peers, slow)),
        dma((chunks, hops)),
        dma((chunks, hops)),
        dma((chunks,)),
        dma((chunks,)),
        dma((half + 1,)),
        dma((half + 1,)),
    ]
    anywhere = pl.BlockSpec(memory_space=pl.ANY)
    inside = pl.BlockSpec(memory_space=pltpu.VMEM)
    weight_grad, acts_grad = pl.pallas_call(
        functools.partial(kernel, n, pipe, cap),
        out_shape=(
            vm((half, dc, hidden), BF16),
            vm((tokens, width), BF16),
        ),
        in_specs=[anywhere] * 4,
        out_specs=(inside, inside),
        scratch_shapes=scratch,
        compiler_params=pltpu.CompilerParams(
            collective_id=0, has_side_effects=True, vmem_limit_bytes=56 * 1024 * 1024
        ),
        cost_estimate=pl.CostEstimate(
            flops=6 * slots * width * hidden,
            bytes_accessed=3 * width * hidden + 4 * tokens * width,
            transcendentals=slots * hidden,
        ),
    )(routes, acts, weight, cot)
    return (weight_grad.reshape(1, width // 2, hidden), acts_grad[None, None])


def solution(mesh):
    return jax.shard_map(
        per_device,
        mesh=mesh,
        in_specs=(
            P("pipe", "rep", "fsdp", None),
            P("pipe", "rep", "fsdp", None),
            P("pipe", None, "fsdp"),
            P("pipe", "rep", None, "fsdp"),
        ),
        out_specs=(P("pipe", "rep", "fsdp"), P("pipe", "rep", "fsdp", None)),
        check_vma=False,
    )
```

```python
import functools

import jax
import jax.numpy as jnp
from jax import lax
from jax.experimental import pallas as pl
from jax.experimental.pallas import tpu as pltpu
from jax.sharding import PartitionSpec as P

MESH = pl.DeviceIdType.MESH
F32 = jnp.float32
BF16 = jnp.bfloat16
CHUNKS = 4


def factors(n):
    fast = 1
    while (fast * 2) ** 2 <= n:
        fast *= 2
    return n // fast, fast


def kernel(
    n, pipe, cap,
    routes_hbm, acts_hbm, weight_hbm, cot_hbm,
    w_sum, spread,
    ids, acts, weight, cot, compacted, gathered, rows, rows_out, acc, pre_grad,
    own_term, y_out, y_in, z_out, z_in,
    local_sem, ids_sem, x_send, g_recv, gf_send, y_send, y_recv, z_send, z_recv,
    f_send, f_recv,
):
    chunks = CHUNKS
    slow, fast = factors(n)
    p, f, r = lax.axis_index("pipe"), lax.axis_index("fsdp"), lax.axis_index("rep")
    a, b = f // fast, lax.rem(f, fast)
    nxt, prv = lax.rem(p + 1, pipe), lax.rem(p + pipe - 1, pipe)
    slots = n * cap
    dc = weight.shape[1]
    half = chunks // 2

    def peer(j):
        return a * fast + lax.rem(b + j, fast)

    def ahead(k):
        return lax.rem(a + k, slow)

    def behind(k):
        return lax.rem(a + slow - k, slow)

    def remote(src, dst, send, recv, where):
        return pltpu.make_async_remote_copy(
            src_ref=src, dst_ref=dst, send_sem=send, recv_sem=recv,
            device_id=where, device_id_type=MESH,
        )

    def greet(where):
        pl.semaphore_signal(barrier, inc=1, device_id=where, device_id_type=MESH)

    acts_load = pltpu.make_async_copy(acts_hbm, acts, local_sem.at[0])
    acts_load.start()
    barrier = pltpu.get_barrier_semaphore()
    for k in range(slow):
        greet({"pipe": prv, "fsdp": ahead(k) * fast + b})
        if pipe > 2:
            greet({"pipe": nxt, "fsdp": ahead(k) * fast + b})
    greet({"rep": 1 - r})
    for j in range(1, fast):
        greet({"fsdp": peer(j)})

    weight_loads = []
    for c in range(chunks):
        load = pltpu.make_async_copy(
            weight_hbm.at[pl.ds(c * dc, dc)], weight.at[c], local_sem.at[2 + c]
        )
        load.start()
        weight_loads.append(load)
    cot_load = pltpu.make_async_copy(cot_hbm, cot, local_sem.at[1])
    cot_load.start()

    pl.semaphore_wait(barrier, (1 if pipe == 2 else 2) * slow + fast)

    ids_copy = remote(routes_hbm, ids, ids_sem.at[0], ids_sem.at[1], {"pipe": prv})
    ids_copy.start()
    ids_copy.wait_recv()
    tokens = ids.shape[1]
    named = jnp.where(ids[...] == 0, 1.0, 0.0).astype(F32)
    chosen = jnp.max(named, axis=0, keepdims=True)
    row = lax.broadcasted_iota(jnp.int32, (tokens, tokens), 0)
    col = lax.broadcasted_iota(jnp.int32, (tokens, tokens), 1)
    before = jnp.where(row <= col, 1.0, 0.0).astype(BF16)
    chosen8 = jnp.broadcast_to(chosen, (16, tokens))
    ordinal = jnp.dot(chosen8.astype(BF16), before, preferred_element_type=F32)[0:1] - 1.0
    hits = jnp.where(
        (jnp.broadcast_to(ordinal, (tokens, tokens)) == row.astype(F32))
        & (jnp.broadcast_to(chosen, (tokens, tokens)) > 0.5),
        1.0, 0.0,
    ).astype(F32)
    picker = hits[0:cap].astype(BF16)
    spreader = hits.T.astype(BF16)
    acts_load.wait()

    def x_copy(c, k):
        return remote(
            compacted.at[c], gathered.at[c, f], x_send.at[c, k], g_recv.at[c, f],
            {"pipe": nxt, "fsdp": behind(k) * fast + b},
        )

    for c in range(chunks):
        compacted[c] = jnp.dot(
            picker, acts[:, c * dc:(c + 1) * dc], preferred_element_type=F32
        ).astype(BF16)
        for k in range(slow):
            x_copy(c, k).start()

    def g_wait(c, block):
        remote(
            gathered.at[c, block], gathered.at[c, block],
            x_send.at[c, 0], g_recv.at[c, block], {"pipe": nxt},
        ).wait_recv()

    def fast_copy(c, k, j):
        block = ahead(k) * fast + b
        return remote(
            gathered.at[c, block], gathered.at[c, block], gf_send.at[c, k, j - 1],
            g_recv.at[c, block], {"fsdp": peer(j)},
        )

    def pass_on(c):
        for k in range(slow):
            g_wait(c, ahead(k) * fast + b)
            for j in range(1, fast):
                fast_copy(c, k, j).start()

    def rows_copy(i):
        return remote(rows_out.at[i], rows.at[i, 1], f_send.at[i], f_recv.at[i], {"rep": 1 - r})

    grad_copy = remote(
        pre_grad.at[0], pre_grad.at[1], f_send.at[half], f_recv.at[half], {"rep": 1 - r}
    )

    def first_matmul(c):
        for k in range(slow):
            for j in range(1, fast):
                g_wait(c, ahead(k) * fast + lax.rem(b + j, fast))
        block = gathered[c].astype(F32).reshape(slots, dc).astype(BF16)
        i, mine = c % half, r == c // half

        @pl.when(mine)
        def _():
            rows[i, 0] = block

        @pl.when(jnp.logical_not(mine))
        def _():
            rows_out[i] = block
            rows_copy(i).start()

        weight_loads[c].wait()
        part = jnp.dot(block, weight[c], preferred_element_type=F32)
        if c == 0:
            acc[...] = part
        else:
            acc[...] += part

    pass_on(0)
    for c in range(chunks):
        if c + 1 < chunks:
            pass_on(c + 1)
        first_matmul(c)

    cot_load.wait()
    piece = 48
    for i in range(slots // piece):
        span = pl.ds(i * piece, piece)
        pre = acc[span]
        s = jax.nn.sigmoid(pre)
        pre_grad[0, span] = (cot[span].astype(F32) * s * (1.0 + pre * (1.0 - s))).astype(BF16)
    grad_copy.start()

    def y_copy(c, j, k):
        to, dest = lax.rem(b + j, fast), behind(k)
        return remote(
            y_out.at[c, to, dest], y_in.at[c, j - 1, dest], y_send.at[c, j - 1, k],
            y_recv.at[c, j - 1, k], {"fsdp": peer(j)},
        )

    def slot_matmul(c):
        term = lax.dot_general(
            pre_grad[0], weight[c], (((1,), (1,)), ((), ())), preferred_element_type=F32
        ).reshape(n, cap, dc)
        own_term[c] = term
        for aa in range(slow):
            for bb in range(fast):
                y_out[c, bb, aa] = term[aa * fast + bb].astype(BF16)
        for k in [*range(1, slow), 0]:
            for j in range(1, fast):
                y_copy(c, j, k).start()

    def partial(c, k):
        dest = behind(k)
        value = own_term[c, dest * fast + b]
        for j in range(1, fast):
            y_copy(c, j, k).wait_recv()
            value = value + y_in[c, j - 1, dest].astype(F32)
        return value

    def z_copy(c, k):
        return remote(
            z_out.at[c, k], z_in.at[c, k], z_send.at[c, k], z_recv.at[c, k],
            {"pipe": prv, "fsdp": behind(k) * fast + b},
        )

    def send_partials(c):
        for k in [*range(1, slow), 0]:
            z_out[c, k] = partial(c, k).astype(BF16)
            z_copy(c, k).start()

    parts = 3
    depth = dc // parts

    def weight_tile(i, part):
        if part == 0:
            rows_copy(i).wait_recv()
            if i == 0:
                grad_copy.wait_recv()
        span = slice(part * depth, (part + 1) * depth)
        w_sum[i, span] = lax.dot_general(
            rows[i, :, :, span].reshape(2 * slots, depth), pre_grad[...].reshape(2 * slots, -1),
            (((0,), (0,)), ((), ())), preferred_element_type=F32,
        ).astype(BF16)

    def put_back(c):
        grads = jnp.zeros((cap, dc), F32)
        for k in range(slow):
            z_copy(c, k).wait_recv()
            grads = grads + z_in[c, k].astype(F32)
        grads = grads.astype(BF16).astype(F32)
        padded = jnp.concatenate(
            [grads, jnp.zeros((tokens - cap, dc), F32)], axis=0
        ).astype(BF16)
        spread[:, c * dc:(c + 1) * dc] = jnp.dot(
            spreader, padded, preferred_element_type=F32
        ).astype(BF16)

    beside = [functools.partial(weight_tile, i, j) for i in range(half) for j in range(parts)]
    beside.reverse()
    for c in range(chunks):
        slot_matmul(c)
        if c == chunks - 1:
            beside.pop()()
        if c:
            send_partials(c - 1)
    beside.pop()()
    put_back(0)
    if beside:
        beside.pop()()
    send_partials(chunks - 1)
    for c in range(1, chunks):
        if beside:
            beside.pop()()
        if c == chunks - 1:
            while beside:
                beside.pop()()
        put_back(c)

    ids_copy.wait_send()
    for c in range(chunks):
        for k in range(slow):
            for j in range(1, fast):
                fast_copy(c, k, j).wait_send()
                y_copy(c, j, k).wait_send()
            x_copy(c, k).wait_send()
            z_copy(c, k).wait_send()
    for i in range(half):
        rows_copy(i).wait_send()
    grad_copy.wait_send()


def per_device(section_acts, route_ids, gate_weight, hidden_cot):
    n, pipe = lax.axis_size("fsdp"), lax.axis_size("pipe")
    acts, weight, cot = section_acts[0, 0], gate_weight[0], hidden_cot[0, 0]
    routes = route_ids[0, 0].T
    tokens, width = acts.shape
    slots, hidden = cot.shape
    cap = slots // n
    slow, fast = factors(n)
    chunks, half = CHUNKS, CHUNKS // 2
    dc = width // chunks
    peers = max(fast - 1, 1)
    dma = pltpu.SemaphoreType.DMA
    vm = pltpu.VMEM
    scratch = [
        vm(routes.shape, jnp.int32),
        vm((tokens, width), BF16),
        vm((chunks, dc, hidden), BF16),
        vm((slots, hidden), BF16),
        vm((chunks, cap, dc), BF16),
        vm((chunks, n, cap, dc), BF16),
        vm((half, 2, slots, dc), BF16),
        vm((half, slots, dc), BF16),
        vm((slots, hidden), F32),
        vm((2, slots, hidden), BF16),
        vm((chunks, n, cap, dc), F32),
        vm((chunks, fast, slow, cap, dc), BF16),
        vm((chunks, peers, slow, cap, dc), BF16),
        vm((chunks, slow, cap, dc), BF16),
        vm((chunks, slow, cap, dc), BF16),
        dma((2 + chunks,)),
        dma((2,)),
        dma((chunks, slow)),
        dma((chunks, n)),
        dma((chunks, slow, peers)),
        dma((chunks, peers, slow)),
        dma((chunks, peers, slow)),
        dma((chunks, slow)),
        dma((chunks, slow)),
        dma((half + 1,)),
        dma((half + 1,)),
    ]
    anywhere = pl.BlockSpec(memory_space=pl.ANY)
    inside = pl.BlockSpec(memory_space=pltpu.VMEM)
    weight_grad, acts_grad = pl.pallas_call(
        functools.partial(kernel, n, pipe, cap),
        out_shape=(
            vm((half, dc, hidden), BF16),
            vm((tokens, width), BF16),
        ),
        in_specs=[anywhere] * 4,
        out_specs=(inside, inside),
        scratch_shapes=scratch,
        compiler_params=pltpu.CompilerParams(
            collective_id=0, has_side_effects=True, vmem_limit_bytes=56 * 1024 * 1024
        ),
        cost_estimate=pl.CostEstimate(
            flops=6 * slots * width * hidden,
            bytes_accessed=3 * width * hidden + 4 * tokens * width,
            transcendentals=slots * hidden,
        ),
    )(routes, acts, weight, cot)
    return (weight_grad.reshape(1, width // 2, hidden), acts_grad[None, None])


def solution(mesh):
    return jax.shard_map(
        per_device,
        mesh=mesh,
        in_specs=(
            P("pipe", "rep", "fsdp", None),
            P("pipe", "rep", "fsdp", None),
            P("pipe", None, "fsdp"),
            P("pipe", "rep", None, "fsdp"),
        ),
        out_specs=(P("pipe", "rep", "fsdp"), P("pipe", "rep", "fsdp", None)),
        check_vma=False,
    )
```

```python
import functools

import jax
import jax.numpy as jnp
from jax import lax
from jax.experimental import pallas as pl
from jax.experimental.pallas import tpu as pltpu
from jax.sharding import PartitionSpec as P

MESH = pl.DeviceIdType.MESH
F32 = jnp.float32
BF16 = jnp.bfloat16
CHUNKS = 4


def factors(n):
    fast = 1
    while (fast * 2) ** 2 <= n:
        fast *= 2
    return n // fast, fast


def kernel(
    n, pipe, cap,
    routes_hbm, acts_hbm, weight_hbm, cot_hbm,
    w_sum, spread,
    ids, acts, weight, cot, compacted, gathered, rows, rows_out, acc, pre_grad,
    own_term, w_acc, y_out, y_in, z_out, z_in,
    local_sem, ids_sem, x_send, g_recv, gf_send, y_send, y_recv, z_send, z_recv,
    f_send, f_recv,
):
    chunks = CHUNKS
    slow, fast = factors(n)
    p, f, r = lax.axis_index("pipe"), lax.axis_index("fsdp"), lax.axis_index("rep")
    a, b = f // fast, lax.rem(f, fast)
    nxt, prv = lax.rem(p + 1, pipe), lax.rem(p + pipe - 1, pipe)
    slots = n * cap
    dc = weight.shape[1]
    half = chunks // 2

    def peer(j):
        return a * fast + lax.rem(b + j, fast)

    def ahead(k):
        return lax.rem(a + k, slow)

    def behind(k):
        return lax.rem(a + slow - k, slow)

    def remote(src, dst, send, recv, where):
        return pltpu.make_async_remote_copy(
            src_ref=src, dst_ref=dst, send_sem=send, recv_sem=recv,
            device_id=where, device_id_type=MESH,
        )

    def greet(where):
        pl.semaphore_signal(barrier, inc=1, device_id=where, device_id_type=MESH)

    acts_load = pltpu.make_async_copy(acts_hbm, acts, local_sem.at[0])
    acts_load.start()
    barrier = pltpu.get_barrier_semaphore()
    for k in range(slow):
        greet({"pipe": prv, "fsdp": ahead(k) * fast + b})
        if pipe > 2:
            greet({"pipe": nxt, "fsdp": ahead(k) * fast + b})
    greet({"rep": 1 - r})
    for j in range(1, fast):
        greet({"fsdp": peer(j)})

    weight_loads = []
    for c in range(chunks):
        load = pltpu.make_async_copy(
            weight_hbm.at[pl.ds(c * dc, dc)], weight.at[c], local_sem.at[2 + c]
        )
        load.start()
        weight_loads.append(load)
    cot_load = pltpu.make_async_copy(cot_hbm, cot, local_sem.at[1])
    cot_load.start()

    pl.semaphore_wait(barrier, (1 if pipe == 2 else 2) * slow + fast)

    ids_copy = remote(routes_hbm, ids, ids_sem.at[0], ids_sem.at[1], {"pipe": prv})
    ids_copy.start()
    ids_copy.wait_recv()
    tokens = ids.shape[1]
    named = jnp.where(ids[...] == 0, 1.0, 0.0).astype(F32)
    chosen = jnp.max(named, axis=0, keepdims=True)
    row = lax.broadcasted_iota(jnp.int32, (tokens, tokens), 0)
    col = lax.broadcasted_iota(jnp.int32, (tokens, tokens), 1)
    before = jnp.where(row <= col, 1.0, 0.0).astype(BF16)
    chosen8 = jnp.broadcast_to(chosen, (16, tokens))
    ordinal = jnp.dot(chosen8.astype(BF16), before, preferred_element_type=F32)[0:1] - 1.0
    hits = jnp.where(
        (jnp.broadcast_to(ordinal, (tokens, tokens)) == row.astype(F32))
        & (jnp.broadcast_to(chosen, (tokens, tokens)) > 0.5),
        1.0, 0.0,
    ).astype(F32)
    picker = hits[0:cap].astype(BF16)
    spreader = hits.T.astype(BF16)
    acts_load.wait()

    def x_copy(c, k):
        return remote(
            compacted.at[c], gathered.at[c, f], x_send.at[c, k], g_recv.at[c, f],
            {"pipe": nxt, "fsdp": behind(k) * fast + b},
        )

    for c in range(chunks):
        compacted[c] = jnp.dot(
            picker, acts[:, c * dc:(c + 1) * dc], preferred_element_type=F32
        ).astype(BF16)
        for k in range(slow):
            x_copy(c, k).start()

    def g_wait(c, block):
        remote(
            gathered.at[c, block], gathered.at[c, block],
            x_send.at[c, 0], g_recv.at[c, block], {"pipe": nxt},
        ).wait_recv()

    def fast_copy(c, k, j):
        block = ahead(k) * fast + b
        return remote(
            gathered.at[c, block], gathered.at[c, block], gf_send.at[c, k, j - 1],
            g_recv.at[c, block], {"fsdp": peer(j)},
        )

    def pass_on(c):
        for k in range(slow):
            g_wait(c, ahead(k) * fast + b)
            for j in range(1, fast):
                fast_copy(c, k, j).start()

    def rows_copy(i):
        return remote(rows_out.at[i], rows.at[i, 1], f_send.at[i], f_recv.at[i], {"rep": 1 - r})

    grad_copy = remote(
        pre_grad.at[0], pre_grad.at[1], f_send.at[half], f_recv.at[half], {"rep": 1 - r}
    )

    def first_matmul(c):
        for k in range(slow):
            for j in range(1, fast):
                g_wait(c, ahead(k) * fast + lax.rem(b + j, fast))
        block = gathered[c].astype(F32).reshape(slots, dc).astype(BF16)
        i, mine = c % half, r == c // half

        @pl.when(mine)
        def _():
            rows[i, 0] = block

        @pl.when(jnp.logical_not(mine))
        def _():
            rows_out[i] = block
            rows_copy(i).start()

        weight_loads[c].wait()
        part = jnp.dot(block, weight[c], preferred_element_type=F32)
        if c == 0:
            acc[...] = part
        else:
            acc[...] += part

    pass_on(0)
    for c in range(chunks):
        if c + 1 < chunks:
            pass_on(c + 1)
        first_matmul(c)

    cot_load.wait()
    piece = 48
    for i in range(slots // piece):
        span = pl.ds(i * piece, piece)
        pre = acc[span]
        s = jax.nn.sigmoid(pre)
        pre_grad[0, span] = (cot[span].astype(F32) * s * (1.0 + pre * (1.0 - s))).astype(BF16)
    grad_copy.start()

    def y_copy(c, j, k):
        to, dest = lax.rem(b + j, fast), behind(k)
        return remote(
            y_out.at[c, to, dest], y_in.at[c, j - 1, dest], y_send.at[c, j - 1, k],
            y_recv.at[c, j - 1, k], {"fsdp": peer(j)},
        )

    def slot_matmul(c):
        term = lax.dot_general(
            pre_grad[0], weight[c], (((1,), (1,)), ((), ())), preferred_element_type=F32
        ).reshape(n, cap, dc)
        own_term[c] = term
        for aa in range(slow):
            for bb in range(fast):
                y_out[c, bb, aa] = term[aa * fast + bb].astype(BF16)
        for k in [*range(1, slow), 0]:
            for j in range(1, fast):
                y_copy(c, j, k).start()

    def partial(c, k):
        dest = behind(k)
        value = own_term[c, dest * fast + b]
        for j in range(1, fast):
            y_copy(c, j, k).wait_recv()
            value = value + y_in[c, j - 1, dest].astype(F32)
        return value

    def z_copy(c, k):
        return remote(
            z_out.at[c, k], z_in.at[c, k], z_send.at[c, k], z_recv.at[c, k],
            {"pipe": prv, "fsdp": behind(k) * fast + b},
        )

    def send_partials(c):
        for k in [*range(1, slow), 0]:
            z_out[c, k] = partial(c, k).astype(BF16)
            z_copy(c, k).start()

    parts = 3 if dc % 3 == 0 else 1
    depth = dc // parts

    def product(i, which, span):
        return lax.dot_general(
            rows[i, which, :, span], pre_grad[which], (((0,), (0,)), ((), ())),
            preferred_element_type=F32,
        )

    def own_tile(i, part):
        span = slice(part * depth, (part + 1) * depth)
        w_acc[i, span] = product(i, 0, span)

    def other_tile(i, part):
        if part == 0:
            rows_copy(i).wait_recv()
            if i == 0:
                grad_copy.wait_recv()
        span = slice(part * depth, (part + 1) * depth)
        w_sum[i, span] = (w_acc[i, span] + product(i, 1, span)).astype(BF16)

    def put_back(c):
        grads = jnp.zeros((cap, dc), F32)
        for k in range(slow):
            z_copy(c, k).wait_recv()
            grads = grads + z_in[c, k].astype(F32)
        grads = grads.astype(BF16).astype(F32)
        padded = jnp.concatenate(
            [grads, jnp.zeros((tokens - cap, dc), F32)], axis=0
        ).astype(BF16)
        spread[:, c * dc:(c + 1) * dc] = jnp.dot(
            spreader, padded, preferred_element_type=F32
        ).astype(BF16)

    tiles = [(i, j) for i in range(half) for j in range(parts)]
    own = [functools.partial(own_tile, *tile) for tile in reversed(tiles)]
    others = [functools.partial(other_tile, *tile) for tile in reversed(tiles)]
    for c in range(chunks):
        slot_matmul(c)
        if c:
            own.pop()()
            send_partials(c - 1)
    own.pop()()
    send_partials(chunks - 1)
    while own:
        own.pop()()
    for c in range(chunks):
        share = 1 if c == 0 else 2
        for _ in range(len(others) if c == chunks - 1 else min(share, len(others))):
            others.pop()()
        put_back(c)

    ids_copy.wait_send()
    for c in range(chunks):
        for k in range(slow):
            for j in range(1, fast):
                fast_copy(c, k, j).wait_send()
                y_copy(c, j, k).wait_send()
            x_copy(c, k).wait_send()
            z_copy(c, k).wait_send()
    for i in range(half):
        rows_copy(i).wait_send()
    grad_copy.wait_send()


def per_device(section_acts, route_ids, gate_weight, hidden_cot):
    n, pipe = lax.axis_size("fsdp"), lax.axis_size("pipe")
    acts, weight, cot = section_acts[0, 0], gate_weight[0], hidden_cot[0, 0]
    routes = route_ids[0, 0].T
    tokens, width = acts.shape
    slots, hidden = cot.shape
    cap = slots // n
    slow, fast = factors(n)
    chunks, half = CHUNKS, CHUNKS // 2
    dc = width // chunks
    peers = max(fast - 1, 1)
    dma = pltpu.SemaphoreType.DMA
    vm = pltpu.VMEM
    scratch = [
        vm(routes.shape, jnp.int32),
        vm((tokens, width), BF16),
        vm((chunks, dc, hidden), BF16),
        vm((slots, hidden), BF16),
        vm((chunks, cap, dc), BF16),
        vm((chunks, n, cap, dc), BF16),
        vm((half, 2, slots, dc), BF16),
        vm((half, slots, dc), BF16),
        vm((slots, hidden), F32),
        vm((2, slots, hidden), BF16),
        vm((chunks, n, cap, dc), F32),
        vm((half, dc, hidden), F32),
        vm((chunks, fast, slow, cap, dc), BF16),
        vm((chunks, peers, slow, cap, dc), BF16),
        vm((chunks, slow, cap, dc), BF16),
        vm((chunks, slow, cap, dc), BF16),
        dma((2 + chunks,)),
        dma((2,)),
        dma((chunks, slow)),
        dma((chunks, n)),
        dma((chunks, slow, peers)),
        dma((chunks, peers, slow)),
        dma((chunks, peers, slow)),
        dma((chunks, slow)),
        dma((chunks, slow)),
        dma((half + 1,)),
        dma((half + 1,)),
    ]
    anywhere = pl.BlockSpec(memory_space=pl.ANY)
    inside = pl.BlockSpec(memory_space=pltpu.VMEM)
    weight_grad, acts_grad = pl.pallas_call(
        functools.partial(kernel, n, pipe, cap),
        out_shape=(
            vm((half, dc, hidden), BF16),
            vm((tokens, width), BF16),
        ),
        in_specs=[anywhere] * 4,
        out_specs=(inside, inside),
        scratch_shapes=scratch,
        compiler_params=pltpu.CompilerParams(
            collective_id=0, has_side_effects=True, vmem_limit_bytes=56 * 1024 * 1024
        ),
        cost_estimate=pl.CostEstimate(
            flops=6 * slots * width * hidden,
            bytes_accessed=3 * width * hidden + 4 * tokens * width,
            transcendentals=slots * hidden,
        ),
    )(routes, acts, weight, cot)
    return (weight_grad.reshape(1, width // 2, hidden), acts_grad[None, None])


def solution(mesh):
    return jax.shard_map(
        per_device,
        mesh=mesh,
        in_specs=(
            P("pipe", "rep", "fsdp", None),
            P("pipe", "rep", "fsdp", None),
            P("pipe", None, "fsdp"),
            P("pipe", "rep", None, "fsdp"),
        ),
        out_specs=(P("pipe", "rep", "fsdp"), P("pipe", "rep", "fsdp", None)),
        check_vma=False,
    )
```
